256 devices in a mesh: expert: 8 (over x_hi, y), tensor: 32 (over z, x_lo, core).
Axes of the slice: x: 4 (x_hi: 2, x_lo: 2; x = x_hi * 2 + x_lo), y: 4, z: 8, core: 2. Of those that a mesh axis runs over, the one named last changes fastest.
Arguments:
- tokens: bfloat16 [4096, 3072], P('tensor'), may hold values from -6 to 6
- routes: int32 [4096, 2], P('tensor'), may hold values from 0 to 7, all different within a row; in each aligned block of 128 rows (0 to 127, 128 to 255, ...) at most 40 rows name the same one
- gates: float32 [4096, 2], P('tensor'), may hold values from 0.2 to 1
- gate_w: bfloat16 [8, 16384, 3072], P(None, ('expert', 'tensor')), may hold values from -0.109375 to 0.109375
- up_w: bfloat16 [8, 16384, 3072], P(None, ('expert', 'tensor')), may hold values from -0.109375 to 0.109375
- down_w: bfloat16 [8, 16384, 3072], P(None, ('expert', 'tensor')), may hold values from -0.046875 to 0.046875
Outputs:
- mixed: bfloat16 [4096, 3072], P('tensor')
The draws below stay inside these ranges and needn't reach their ends.
Inputs may be any that keep to these rules, and one draw needn't show every extreme that they name: `routes`: in each aligned block of 128 rows (the rows of one tensor index) the 2 experts of a row differ, no expert is named by more than 40 rows, a bound that some block reaches.
All inputs are finite; a program needn't handle non-finite values.
Results may differ from the reference program's by a relative error of at most 0.0058.
Values may be sent and summed in bfloat16 or wider, within the bound.
No kernel may reach another device: no remote copies, remote signals or barrier semaphores. Data moves between devices by JAX's collectives and lax.ppermute only.
A program may use at most 128 MiB of HBM per device.

```python
import math
import jax
import jax.numpy as jnp
import numpy as np
from jax import lax

D = 3072
FF = 16384
TOP = 2
TOK_DEV = 128
EXPERTS = 8
TOKENS = 4096
CAP = 40
BLOCK = 64
N_TENSOR = 32


def levels(own_key, dims, split, least, high):
    level, own = 1.0, jax.random.fold_in(own_key, 6)
    for axis_at, shards_of in split:
        steps = jnp.exp(jax.random.uniform(jax.random.fold_in(own, axis_at), (shards_of,), jnp.float32, least / len(split), high / len(split)))
        level = level * jnp.repeat(steps, dims[axis_at] // shards_of).reshape([-1 if axis == axis_at else 1 for axis in range(len(dims))])
    return level


def deal_out(stream_key, own, number, rows, amount, top, bound, slope):
    sequence = jax.random.permutation(stream_key, amount)
    crowded, usual = portions_of(amount, rows * top, bound, slope, True), portions_of(amount, rows * top, bound, slope, False)
    places = jnp.arange(amount)

    def named(lengths, turn):
        used = int((lengths > 0).sum())
        fixed = max(1, used // 4)
        shifted = fixed + (places - fixed + turn * (used - fixed)) % max(1, amount - fixed)
        return jnp.zeros((amount,), jnp.int32).at[sequence[jnp.where(places < fixed, places, shifted)]].set(jnp.asarray(lengths, jnp.int32))

    lengths = jnp.where(number % 4 == 0, named(crowded, number // 4), named(usual, number - number // 4 - 1))
    mixed = jax.random.permutation(jax.random.fold_in(own, 3), amount)
    source_of, sink = mixed[0:amount // 2 * 2:2], mixed[1:amount // 2 * 2:2]
    margin = jnp.minimum(lengths[source_of] - 1, bound - lengths[sink]) // 2
    margin = jnp.where((source_of == sequence[0]) | (sink == sequence[0]) | (lengths[sink] == 0), 0, jnp.maximum(margin, 0))
    shifted = jax.random.randint(jax.random.fold_in(own, 4), (amount // 2,), 0, 1 << 20) % (margin + 1)
    lengths = lengths.at[source_of].add(-shifted).at[sink].add(shifted)
    items = jnp.searchsorted(jnp.cumsum(lengths), jnp.arange(rows * top), side="right").astype(jnp.int32)
    grid = items.reshape(top, rows).T
    grid = grid[jax.random.permutation(jax.random.fold_in(own, 1), rows)]
    turn = jax.random.randint(jax.random.fold_in(own, 2), (rows, 1), 0, top)
    return jnp.take_along_axis(grid, (jnp.arange(top)[None, :] + turn) % top, axis=1)


def portions_of(amount, total, limit, lean, full):
    weights = [(1 << 20) // math.isqrt(grade ** lean) + 1 for grade in range(1, amount + 1)]
    largest = limit if full else min(limit, max(-(-total // amount), total * weights[0] // sum(weights)))
    least = 1 if total - largest >= amount - 1 else 0
    counts, spare = [largest] + [least] * (amount - 1), total - largest - least * (amount - 1)
    while spare > 0:
        movable = [i for i in range(1, amount) if counts[i] < largest] or [i for i in range(1, amount) if counts[i] < limit]
        mass, remaining = sum([weights[i] for i in movable]), spare
        for i in movable:
            extra = min(limit - counts[i], max(1, remaining * weights[i] // mass), spare)
            counts[i] = counts[i] + extra
            spare = spare - extra
    return np.array(counts)


def centred(stream_key, shape, spread, bound, pieces=(), held_as=jnp.bfloat16):
    result = spread * jax.random.normal(stream_key, shape, jnp.float32)
    if pieces:
        result = result * levels(stream_key, shape, pieces, -0.22, 0.18)
    return jnp.clip(result, -bound, bound).astype(held_as)


def setup_inputs(seed: int = 0) -> dict:
    splits = jax.random.split(jax.random.key(seed), 7)
    tokens = centred(splits[0], (TOKENS, D), 1.0, 6.0, ((0, 32),))
    routes_keys = jax.random.split(jax.random.fold_in(splits[1], 1), TOKENS // TOK_DEV)
    routes_turns = jax.random.permutation(jax.random.fold_in(splits[1], 3), TOKENS // TOK_DEV)
    routes = jax.vmap(lambda own, number: deal_out(jax.random.fold_in(splits[1], 2), own, number, TOK_DEV, EXPERTS, TOP, CAP, 2))(routes_keys, routes_turns).reshape((TOKENS, TOP))
    gates = jnp.clip(0.2 + 0.8 * jax.random.uniform(splits[2], (TOKENS, TOP), jnp.float32) ** levels(splits[2], (TOKENS, TOP), ((0, 32),), -0.2, 0.2), 0.2, 1.0)
    gate_w = centred(splits[3], (EXPERTS, FF, D), D ** -0.5, 0.109375, ((1, 256),))
    up_w = centred(splits[4], (EXPERTS, FF, D), D ** -0.5, 0.109375, ((1, 256),))
    down_w = centred(splits[5], (EXPERTS, FF, D), FF ** -0.5, 0.046875, ((1, 256),))
    return dict(tokens=tokens, routes=routes, gates=gates, gate_w=gate_w, up_w=up_w, down_w=down_w)


def slot_tables(routes, gates, expert_count, capacity):
    labels = jnp.arange(expert_count, dtype=jnp.int32)
    matches_all = routes[None, :, :] == labels[:, None, None]
    member = jnp.any(matches_all, axis=2)
    weight = jnp.sum(jnp.where(matches_all, gates[None, :, :], jnp.zeros_like(gates)[None, :, :]), axis=2)
    position = jnp.cumsum(member.astype(jnp.int32), axis=1) - 1
    places = jnp.arange(capacity, dtype=jnp.int32)
    onehot = jnp.logical_and(position[:, None, :] == places[None, :, None], member[:, None, :])
    return onehot.astype(jnp.float32), weight


def swiglu(selected, gate_matrix, up_matrix):
    contract = (((1,), (1,)), ((), ()))
    gated = lax.dot_general(selected, gate_matrix, contract, preferred_element_type=jnp.float32)
    upward = lax.dot_general(selected, up_matrix, contract, preferred_element_type=jnp.float32)
    return (jax.nn.silu(gated) * upward).astype(jnp.bfloat16)


def reference(tokens, routes, gates, gate_w, up_w, down_w):
    members = N_TENSOR
    owner_rows = tokens.reshape(members, TOK_DEV, D)
    onehot, weight = jax.vmap(lambda r, g: slot_tables(r, g, EXPERTS, CAP))(
        routes.reshape(members, TOK_DEV, TOP), gates.reshape(members, TOK_DEV, TOP))

    def one_expert(running, expert):
        chosen = onehot[:, expert]
        selected = jnp.einsum("nct,ntd->ncd", chosen, owner_rows.astype(jnp.float32),
                              precision=lax.Precision.HIGHEST).astype(jnp.bfloat16).reshape(members * CAP, D)
        hidden = swiglu(selected, gate_w[expert], up_w[expert])
        sliced = hidden.reshape(members * CAP, EXPERTS, members, BLOCK).transpose(2, 0, 1, 3)
        down_parts = down_w[expert].reshape(EXPERTS, members, BLOCK, D).transpose(1, 0, 2, 3)

        def add_part(summed, couple):
            segment, matrix = couple
            product = jnp.dot(segment.reshape(members * CAP, EXPERTS * BLOCK),
                              matrix.reshape(EXPERTS * BLOCK, D), preferred_element_type=jnp.float32)
            return summed + product, None

        summed, _ = lax.scan(add_part, jnp.zeros((members * CAP, D), jnp.float32), (sliced, down_parts))
        expert_out = summed.astype(jnp.bfloat16).reshape(members, CAP, D)
        scaled = chosen * weight[:, expert][:, None, :]
        placed = jnp.einsum("nct,ncd->ntd", scaled, expert_out.astype(jnp.float32),
                            precision=lax.Precision.HIGHEST)
        return running + placed, None

    running, _ = lax.scan(one_expert, jnp.zeros((members, TOK_DEV, D), jnp.float32),
                          jnp.arange(EXPERTS, dtype=jnp.int32))
    return running.reshape(TOKENS, D).astype(jnp.bfloat16)
```

```python
import jax
import jax.numpy as jnp
from jax import lax
from jax.sharding import PartitionSpec as P

CHUNKS = 2


def slot_tables(routes, gates, expert_count, capacity):
    labels = jnp.arange(expert_count, dtype=jnp.int32)
    matches_all = routes[None, :, :] == labels[:, None, None]
    member = jnp.any(matches_all, axis=2)
    weight = jnp.sum(
        jnp.where(matches_all, gates[None, :, :], jnp.zeros_like(gates)[None, :, :]), axis=2
    )
    position = jnp.cumsum(member.astype(jnp.int32), axis=1) - 1
    places = jnp.arange(capacity, dtype=jnp.int32)
    onehot = jnp.logical_and(position[:, None, :] == places[None, :, None], member[:, None, :])
    return (onehot.astype(jnp.float32), weight)


def along_z(step):
    return [(t, (t + 4 * step) % 32) for t in range(32)]


X_LO = [(t, t ^ 2) for t in range(32)]
CORE = [(t, t ^ 1) for t in range(32)]


def expert_partner(e, k):
    return ((e // 4) ^ (k // 4)) * 4 + (e % 4 + k) % 4


def add(a, b):
    return a.astype(jnp.float32) + b.astype(jnp.float32)


def per_device(tokens, routes, gates, gate_w, up_w, down_w):
    expert_count = lax.axis_size("expert")
    tok_rows, width = tokens.shape
    capacity = 5 * tok_rows * routes.shape[1] // (4 * expert_count)
    expert = lax.axis_index("expert")
    bf16 = jnp.bfloat16

    def tensor_move(value, pairs):
        return lax.ppermute(value, "tensor", pairs)

    with jax.named_scope("pick"):
        onehot, weight = slot_tables(routes, gates, expert_count, capacity)
        chosen = lax.dynamic_index_in_dim(onehot, expert, 0, keepdims=False)
        picked = jnp.dot(
            chosen.astype(bf16), tokens, preferred_element_type=jnp.float32
        ).astype(bf16)

    with jax.named_scope("weights"):
        gate_own = lax.all_to_all(gate_w, "expert", split_axis=0, concat_axis=1, tiled=True)[0]
        up_own = lax.all_to_all(up_w, "expert", split_axis=0, concat_axis=1, tiled=True)[0]

    with jax.named_scope("gather_rows"):
        own = jnp.concatenate([picked, tensor_move(picked, X_LO)], axis=0)
        blocks = [own] + [None] * 7
        up_going, down_going = own, own
        for k in (1, 2, 3):
            down_going = tensor_move(down_going, along_z(-1))
            up_going = tensor_move(up_going, along_z(1))
            blocks[k], blocks[8 - k] = down_going, up_going
        half = width // 2
        blocks[4] = jnp.concatenate(
            [
                tensor_move(down_going[:, :half], along_z(-1)),
                tensor_move(up_going[:, half:], along_z(1)),
            ],
            axis=1,
        )
        mine = jnp.concatenate(blocks, axis=0)
        rows = jnp.concatenate([mine, tensor_move(mine, CORE)], axis=0)

    with jax.named_scope("hidden"):
        contract = (((1,), (1,)), ((), ()))
        gated = lax.dot_general(rows, gate_own, contract, preferred_element_type=jnp.float32)
        upward = lax.dot_general(rows, up_own, contract, preferred_element_type=jnp.float32)
        hidden = (jax.nn.silu(gated) * upward).astype(bf16)

    own_rows = mine.shape[0]
    block = 2 * capacity
    cols = width // CHUNKS
    outs = []
    for n in range(CHUNKS):
        with jax.named_scope(f"down{n}"):
            down_own = lax.all_to_all(
                down_w[:, :, n * cols : (n + 1) * cols],
                "expert",
                split_axis=0,
                concat_axis=1,
                tiled=True,
            )[0]
            theirs = jnp.dot(
                hidden[own_rows:], down_own, preferred_element_type=jnp.float32
            ).astype(bf16)
            mine = jnp.dot(hidden[:own_rows], down_own, preferred_element_type=jnp.float32)
        with jax.named_scope(f"scatter{n}"):
            total = (mine + tensor_move(theirs, CORE).astype(jnp.float32)).astype(bf16)
            parts = [total[k * block : (k + 1) * block] for k in range(8)]
            half = cols // 2
            going_up = tensor_move(parts[4][:, :half], along_z(1))
            going_down = tensor_move(parts[4][:, half:], along_z(-1))
            zeros = jnp.zeros((block, half), bf16)
            going_up = jnp.concatenate([going_up, zeros], axis=1)
            going_down = jnp.concatenate([zeros, going_down], axis=1)
            for k in (3, 2, 1):
                going_up = tensor_move(add(going_up, parts[k]).astype(bf16), along_z(1))
                going_down = tensor_move(add(going_down, parts[8 - k]).astype(bf16), along_z(-1))
            summed = add(going_up, parts[0]) + going_down.astype(jnp.float32)
            far = tensor_move(summed[capacity:].astype(bf16), X_LO)
            expert_out = (summed[:capacity] + far.astype(jnp.float32)).astype(bf16)
        with jax.named_scope(f"spread{n}"):
            spread = [expert_out] + [
                lax.ppermute(
                    expert_out, "expert", [(expert_partner(e, k), e) for e in range(8)]
                )
                for k in range(1, 8)
            ]
            outs.append(jnp.concatenate(spread, axis=0))

    with jax.named_scope("mix"):
        scaled = onehot * weight[:, None, :]
        ks = jnp.arange(8, dtype=jnp.int32)
        partners = ((expert // 4) ^ (ks // 4)) * 4 + (expert % 4 + ks) % 4
        scaled = jnp.take(scaled, partners, axis=0).reshape(8 * capacity, tok_rows)
        mixed = [
            lax.dot_general(
                scaled,
                out.astype(jnp.float32),
                (((0,), (0,)), ((), ())),
                precision=lax.Precision.HIGHEST,
                preferred_element_type=jnp.float32,
            ).astype(bf16)
            for out in outs
        ]
        return jnp.concatenate(mixed, axis=1)


def solution(mesh):
    placed = (
        P("tensor", None),
        P("tensor", None),
        P("tensor", None),
        P(None, ("expert", "tensor"), None),
        P(None, ("expert", "tensor"), None),
        P(None, ("expert", "tensor"), None),
    )
    return jax.shard_map(
        per_device, mesh=mesh, in_specs=placed, out_specs=P("tensor", None), check_vma=False
    )
```

```python
import jax
import jax.numpy as jnp
from jax import lax
from jax.sharding import PartitionSpec as P

CHUNKS = 2


def slot_tables(routes, gates, expert_count, capacity):
    labels = jnp.arange(expert_count, dtype=jnp.int32)
    matches_all = routes[None, :, :] == labels[:, None, None]
    member = jnp.any(matches_all, axis=2)
    weight = jnp.sum(
        jnp.where(matches_all, gates[None, :, :], jnp.zeros_like(gates)[None, :, :]), axis=2
    )
    position = jnp.cumsum(member.astype(jnp.int32), axis=1) - 1
    places = jnp.arange(capacity, dtype=jnp.int32)
    onehot = jnp.logical_and(position[:, None, :] == places[None, :, None], member[:, None, :])
    return (onehot.astype(jnp.float32), weight)


def along_z(step, flip=0):
    return [(t, ((t ^ flip) + 4 * step) % 32) for t in range(32)]


X_LO = [(t, t ^ 2) for t in range(32)]
CORE = [(t, t ^ 1) for t in range(32)]


def add(a, b):
    return a.astype(jnp.float32) + b.astype(jnp.float32)


def product(rows, matrix):
    contract = (((1,), (1,)), ((), ()))
    return lax.dot_general(rows, matrix, contract, preferred_element_type=jnp.float32)


def per_device(tokens, routes, gates, gate_w, up_w, down_w):
    expert_count = lax.axis_size("expert")
    tok_rows, width = tokens.shape
    capacity = 5 * tok_rows * routes.shape[1] // (4 * expert_count)
    expert = lax.axis_index("expert")
    bf16 = jnp.bfloat16

    def tensor_move(value, pairs):
        return lax.ppermute(value, "tensor", pairs)

    def to_groups(matrix):
        return lax.all_to_all(matrix, "expert", split_axis=0, concat_axis=1, tiled=True)[0]

    with jax.named_scope("pick"):
        onehot, weight = slot_tables(routes, gates, expert_count, capacity)
        chosen = lax.dynamic_index_in_dim(onehot, expert, 0, keepdims=False)
        picked = jnp.dot(
            chosen.astype(bf16), tokens, preferred_element_type=jnp.float32
        ).astype(bf16)
        own = jnp.concatenate([picked, tensor_move(picked, X_LO)], axis=0)
        own, gate_w = lax.optimization_barrier((own, gate_w))

    unit = own.shape[0]
    half = width // 2
    with jax.named_scope("gate"):
        gate_own = to_groups(gate_w)
        block = {0: own}
        for k in (1, -1, 2, -2):
            block[k] = tensor_move(own, along_z(-k))
        near = jnp.concatenate([block[k] for k in (0, 1, -1, 2, -2)], axis=0)
        gate_own, near, up_w, down_w = lax.optimization_barrier((gate_own, near, up_w, down_w))

    with jax.named_scope("up"):
        up_own = to_groups(up_w)
        ahead, behind = near[3 * unit : 4 * unit], near[4 * unit :]
        far = (
            tensor_move(ahead, along_z(-1)),
            tensor_move(behind, along_z(1)),
            tensor_move(ahead[:, :half], along_z(-2)),
            tensor_move(behind[:, half:], along_z(2)),
        )
        near = jnp.concatenate([near, tensor_move(near, CORE)], axis=0)
        near_gated = jax.nn.silu(product(near, gate_own))
        far, near, near_gated = lax.optimization_barrier((far, near, near_gated))
        far = jnp.concatenate([far[0], far[1], jnp.concatenate(far[2:], axis=1)], axis=0)
        up_own, near, near_gated, far, down_w = lax.optimization_barrier(
            (up_own, near, near_gated, far, down_w)
        )

    with jax.named_scope("hidden"):
        down_own = to_groups(down_w)
        near_hidden = (near_gated * product(near, up_own)).astype(bf16)
        far_rows = jnp.concatenate([far, tensor_move(far, CORE)], axis=0)
        far_gated = jax.nn.silu(product(far_rows, gate_own))
        far_hidden = (far_gated * product(far_rows, up_own)).astype(bf16)
        n, f = near.shape[0] // 2, far.shape[0]
        hidden_mine = jnp.concatenate([near_hidden[:n], far_hidden[:f]], axis=0)
        hidden_theirs = jnp.concatenate([near_hidden[n:], far_hidden[f:]], axis=0)
        down_own, hidden_mine, hidden_theirs = lax.optimization_barrier(
            (down_own, hidden_mine, hidden_theirs)
        )

    order = (0, 1, -1, 2, -2, 3, -3, 4)

    columns = jnp.split(down_own, CHUNKS, axis=1)
    with jax.named_scope("down"):
        theirs = [
            jnp.dot(hidden_theirs, c, preferred_element_type=jnp.float32).astype(bf16)
            for c in columns
        ]
        received = [tensor_move(t, CORE) for t in theirs]
        hidden_mine, _ = lax.optimization_barrier((hidden_mine, theirs))
        parts = []
        for c, got in zip(columns, received):
            mine = jnp.dot(hidden_mine, c, preferred_element_type=jnp.float32)
            total = (mine + got.astype(jnp.float32)).astype(bf16)
            parts.append({k: total[i * unit : (i + 1) * unit] for i, k in enumerate(order)})

    outs = []
    for n, part in enumerate(parts):
        with jax.named_scope(f"scatter{n}"):
            longer = 1 if n % 2 == 0 else -1
            moving = {longer: tensor_move(part[4], along_z(longer))}
            for k in (3, 2):
                for way in (longer, -longer):
                    here = part[way * k]
                    if way in moving:
                        here = add(moving[way], here).astype(bf16)
                    moving[way] = tensor_move(here, along_z(way))
            summed = part[0][:capacity].astype(jnp.float32)
            summed = add(summed, tensor_move(part[0][capacity:], X_LO))
            for way in (longer, -longer):
                here = add(moving[way], part[way]).astype(bf16)
                summed = add(summed, tensor_move(here[:capacity], along_z(way)))
                summed = add(summed, tensor_move(here[capacity:], along_z(way, 2)))
            expert_out = summed.astype(bf16)
        with jax.named_scope(f"spread{n}"):
            copies = jnp.broadcast_to(expert_out[None], (8,) + expert_out.shape)
            outs.append(to_groups(copies))

    with jax.named_scope("mix"):
        scaled = onehot * weight[:, None, :]
        mixed = []
        spots = scaled.reshape(8 * capacity, tok_rows)
        for out in outs:
            mixed.append(
                lax.dot_general(
                    spots,
                    out.astype(jnp.float32),
                    (((0,), (0,)), ((), ())),
                    precision=lax.Precision.HIGHEST,
                    preferred_element_type=jnp.float32,
                ).astype(bf16)
            )
        return jnp.concatenate(mixed, axis=1)


def solution(mesh):
    placed = (
        P("tensor", None),
        P("tensor", None),
        P("tensor", None),
        P(None, ("expert", "tensor"), None),
        P(None, ("expert", "tensor"), None),
        P(None, ("expert", "tensor"), None),
    )
    return jax.shard_map(
        per_device, mesh=mesh, in_specs=placed, out_specs=P("tensor", None), check_vma=False
    )
```

```python
import jax
import jax.numpy as jnp
from jax import lax
from jax.experimental import pallas as pl
from jax.experimental.pallas import tpu as pltpu
from jax.sharding import PartitionSpec as P

CHUNKS = (1536, 1536)
EARLY = 32
ROW_TILE = 640


def slot_tables(routes, gates, expert_count, capacity):
    labels = jnp.arange(expert_count, dtype=jnp.int32)
    matches_all = routes[None, :, :] == labels[:, None, None]
    member = jnp.any(matches_all, axis=2)
    weight = jnp.sum(
        jnp.where(matches_all, gates[None, :, :], jnp.zeros_like(gates)[None, :, :]), axis=2
    )
    position = jnp.cumsum(member.astype(jnp.int32), axis=1) - 1
    places = jnp.arange(capacity, dtype=jnp.int32)
    onehot = jnp.logical_and(position[:, None, :] == places[None, :, None], member[:, None, :])
    return (onehot.astype(jnp.float32), weight)


def along_z(step, flip=0):
    return [(t, ((t ^ flip) + 4 * step) % 32) for t in range(32)]


X_LO = [(t, t ^ 2) for t in range(32)]
CORE = [(t, t ^ 1) for t in range(32)]


X_HI = [(e, e ^ 4) for e in range(8)]


def from_y(step):
    return [(e // 4 * 4 + (e % 4 + step) % 4, e) for e in range(8)]


def add(a, b):
    return a.astype(jnp.float32) + b.astype(jnp.float32)


def swiglu_kernel(rows_ref, gate_ref, up_ref, out_ref):
    contract = (((1,), (1,)), ((), ()))
    rows = rows_ref[...]
    gate = gate_ref[...].reshape(-1, rows.shape[1])
    up = up_ref[...].reshape(-1, rows.shape[1])
    gated = lax.dot_general(rows, gate, contract, preferred_element_type=jnp.float32)
    upward = lax.dot_general(rows, up, contract, preferred_element_type=jnp.float32)
    out_ref[...] = (gated / (1.0 + jnp.exp(-gated)) * upward).astype(out_ref.dtype)


def swiglu(rows, weights, depth):
    count, width = rows.shape
    sources = weights.shape[0] // 2
    step = sources * depth
    return pl.pallas_call(
        swiglu_kernel,
        grid=(2, count // ROW_TILE),
        in_specs=[
            pl.BlockSpec((ROW_TILE, width), lambda i, j: (j, 0)),
            pl.BlockSpec((sources, depth, width), lambda i, j: (i, 0, 0)),
            pl.BlockSpec((sources, depth, width), lambda i, j: (i, 1, 0)),
        ],
        out_specs=pl.BlockSpec((ROW_TILE, step), lambda i, j: (j, i)),
        out_shape=jax.ShapeDtypeStruct((count, 2 * step), rows.dtype),
        compiler_params=pltpu.CompilerParams(vmem_limit_bytes=60 * 2**20),
        cost_estimate=pl.CostEstimate(flops=1000, bytes_accessed=1000, transcendentals=0),
    )(rows, weights, weights)


def per_device(tokens, routes, gates, gate_w, up_w, down_w):
    expert_count = lax.axis_size("expert")
    tok_rows, width = tokens.shape
    capacity = 5 * tok_rows * routes.shape[1] // (4 * expert_count)
    expert = lax.axis_index("expert")
    bf16 = jnp.bfloat16

    def tensor_move(value, pairs):
        return lax.ppermute(value, "tensor", pairs)

    def expert_move(value, pairs):
        return lax.ppermute(value, "expert", pairs)

    def to_groups(matrix):
        return lax.all_to_all(matrix, "expert", split_axis=0, concat_axis=1, tiled=True)[0]

    with jax.named_scope("pick"):
        onehot, weight = slot_tables(routes, gates, expert_count, capacity)
        chosen = lax.dynamic_index_in_dim(onehot, expert, 0, keepdims=False)
        picked = jnp.dot(
            chosen.astype(bf16), tokens, preferred_element_type=jnp.float32
        ).astype(bf16)
        own = jnp.concatenate([picked, tensor_move(picked, X_LO)], axis=0)
        early = jnp.concatenate([gate_w, up_w, down_w[:, :EARLY]], axis=1)
        own, early, down_w = lax.optimization_barrier((own, early, down_w))

    unit = own.shape[0]
    half = width // 2
    with jax.named_scope("gate_up"):
        early = to_groups(early)
        late = down_w[:, EARLY:]
        block = {0: own}
        for k in (1, -1, 2, -2):
            block[k] = tensor_move(own, along_z(-k))
        block[3] = tensor_move(block[2], along_z(-1))
        block[-3] = tensor_move(block[-2], along_z(1))
        block[4] = jnp.concatenate(
            [
                tensor_move(block[2][:, :half], along_z(-2)),
                tensor_move(block[-2][:, half:], along_z(2)),
            ],
            axis=1,
        )
        order = (0, 1, -1, 2, -2, 3, -3, 4)
        near = jnp.concatenate([block[k] for k in order[:5]], axis=0)
        far = jnp.concatenate([block[k] for k in order[5:]], axis=0)
        rows = jnp.concatenate(
            [near, far, tensor_move(near, CORE), tensor_move(far, CORE)], axis=0
        )
        early, rows, late = lax.optimization_barrier((early, rows, late))

    with jax.named_scope("hidden"):
        late = to_groups(late)
        depth = gate_w.shape[1]
        early = early.reshape(expert_count, -1, width)
        hidden = swiglu(rows, early, depth)

        late, hidden = lax.optimization_barrier((late, hidden))
        late = late.reshape(expert_count, -1, width)
        down_own = jnp.concatenate([early[:, 2 * depth :], late], axis=1).reshape(-1, width)

    own_rows = rows.shape[0] // 2
    edges = [sum(CHUNKS[:n]) for n in range(len(CHUNKS) + 1)]
    columns = [down_own[:, a:b] for a, b in zip(edges[:-1], edges[1:])]
    with jax.named_scope("down"):
        theirs = [
            jnp.dot(hidden[own_rows:], c, preferred_element_type=jnp.float32).astype(bf16)
            for c in columns
        ]
        received = [tensor_move(t, CORE) for t in theirs]
        hidden_mine, _ = lax.optimization_barrier((hidden[:own_rows], theirs))
        totals = []
        for c, got in zip(columns, received):
            mine = jnp.dot(hidden_mine, c, preferred_element_type=jnp.float32)
            totals.append((mine + got.astype(jnp.float32)).astype(bf16))

    def chains(total, longer):
        size = total.shape[0] // 8
        part = {k: total[i * size : (i + 1) * size] for i, k in enumerate(order)}
        moving = {longer: tensor_move(part[4], along_z(longer))}
        for k in (3, 2):
            for way in (longer, -longer):
                here = part[way * k]
                if way in moving:
                    here = add(moving[way], here).astype(bf16)
                moving[way] = tensor_move(here, along_z(way))
        summed = part[0][:capacity].astype(jnp.float32)
        summed = add(summed, tensor_move(part[0][capacity:], X_LO))
        for way in (longer, -longer):
            here = add(moving[way], part[way]).astype(bf16)
            summed = add(summed, tensor_move(here[:capacity], along_z(way)))
            summed = add(summed, tensor_move(here[capacity:], along_z(way, 2)))
        return summed.astype(bf16)

    with jax.named_scope("scatter"):
        outs = [chains(t, 1 if n % 2 == 0 else -1) for n, t in enumerate(totals)]

    with jax.named_scope("mix"):
        scaled = onehot * weight[:, None, :]
        expert_out = jnp.concatenate(outs, axis=1)
        copies = jnp.broadcast_to(expert_out[None], (expert_count,) + expert_out.shape)
        return lax.dot_general(
            scaled.reshape(-1, tok_rows),
            to_groups(copies).astype(jnp.float32),
            (((0,), (0,)), ((), ())),
            precision=lax.Precision.HIGHEST,
            preferred_element_type=jnp.float32,
        ).astype(bf16)


def solution(mesh):
    placed = (
        P("tensor", None),
        P("tensor", None),
        P("tensor", None),
        P(None, ("expert", "tensor"), None),
        P(None, ("expert", "tensor"), None),
        P(None, ("expert", "tensor"), None),
    )
    return jax.shard_map(
        per_device, mesh=mesh, in_specs=placed, out_specs=P("tensor", None), check_vma=False
    )
```

```python
import jax
import jax.numpy as jnp
from jax import lax
from jax.experimental import pallas as pl
from jax.experimental.pallas import tpu as pltpu
from jax.sharding import PartitionSpec as P

EARLY = 32
ROW_TILE = 640


def slot_tables(routes, gates, expert_count, capacity):
    labels = jnp.arange(expert_count, dtype=jnp.int32)
    matches_all = routes[None, :, :] == labels[:, None, None]
    member = jnp.any(matches_all, axis=2)
    weight = jnp.sum(
        jnp.where(matches_all, gates[None, :, :], jnp.zeros_like(gates)[None, :, :]), axis=2
    )
    position = jnp.cumsum(member.astype(jnp.int32), axis=1) - 1
    places = jnp.arange(capacity, dtype=jnp.int32)
    onehot = jnp.logical_and(position[:, None, :] == places[None, :, None], member[:, None, :])
    return (onehot.astype(jnp.float32), weight)


def along_z(step, flip=0):
    return [(t, ((t ^ flip) + 4 * step) % 32) for t in range(32)]


X_LO = [(t, t ^ 2) for t in range(32)]
CORE = [(t, t ^ 1) for t in range(32)]


X_HI = [(e, e ^ 4) for e in range(8)]


def from_y(step):
    return [(e // 4 * 4 + (e % 4 + step) % 4, e) for e in range(8)]


def add(a, b):
    return a.astype(jnp.float32) + b.astype(jnp.float32)


def swiglu_kernel(rows_ref, gate_ref, up_ref, out_ref):
    contract = (((1,), (1,)), ((), ()))
    rows = rows_ref[...]
    gate = gate_ref[...].reshape(-1, rows.shape[1])
    up = up_ref[...].reshape(-1, rows.shape[1])
    gated = lax.dot_general(rows, gate, contract, preferred_element_type=jnp.float32)
    upward = lax.dot_general(rows, up, contract, preferred_element_type=jnp.float32)
    out_ref[...] = (gated / (1.0 + jnp.exp(-gated)) * upward).astype(out_ref.dtype)


def swiglu(rows, weights, depth):
    count, width = rows.shape
    sources = weights.shape[0] // 2
    step = sources * depth
    return pl.pallas_call(
        swiglu_kernel,
        grid=(2, count // ROW_TILE),
        in_specs=[
            pl.BlockSpec((ROW_TILE, width), lambda i, j: (j, 0)),
            pl.BlockSpec((sources, depth, width), lambda i, j: (i, 0, 0)),
            pl.BlockSpec((sources, depth, width), lambda i, j: (i, 1, 0)),
        ],
        out_specs=pl.BlockSpec((ROW_TILE, step), lambda i, j: (j, i)),
        out_shape=jax.ShapeDtypeStruct((count, 2 * step), rows.dtype),
        compiler_params=pltpu.CompilerParams(vmem_limit_bytes=60 * 2**20),
        cost_estimate=pl.CostEstimate(flops=1000, bytes_accessed=1000, transcendentals=0),
    )(rows, weights, weights)


def per_device(tokens, routes, gates, gate_w, up_w, down_w):
    expert_count = lax.axis_size("expert")
    tok_rows, width = tokens.shape
    capacity = 5 * tok_rows * routes.shape[1] // (4 * expert_count)
    expert = lax.axis_index("expert")
    bf16 = jnp.bfloat16

    def tensor_move(value, pairs):
        return lax.ppermute(value, "tensor", pairs)

    def expert_move(value, pairs):
        return lax.ppermute(value, "expert", pairs)

    def to_groups(matrix):
        return lax.all_to_all(matrix, "expert", split_axis=0, concat_axis=1, tiled=True)[0]

    with jax.named_scope("pick"):
        onehot, weight = slot_tables(routes, gates, expert_count, capacity)
        chosen = lax.dynamic_index_in_dim(onehot, expert, 0, keepdims=False)
        picked = jnp.dot(
            chosen.astype(bf16), tokens, preferred_element_type=jnp.float32
        ).astype(bf16)
        own = jnp.concatenate([picked, tensor_move(picked, X_LO)], axis=0)
        early = jnp.concatenate([gate_w, up_w, down_w[:, :EARLY]], axis=1)
        own, early, down_w = lax.optimization_barrier((own, early, down_w))

    unit = own.shape[0]
    half = width // 2
    with jax.named_scope("gate_up"):
        early = to_groups(early)
        late = down_w[:, EARLY:]
        block = {0: own}
        for k in (1, -1, 2, -2):
            block[k] = tensor_move(own, along_z(-k))
        block[3] = tensor_move(block[2], along_z(-1))
        block[-3] = tensor_move(block[-2], along_z(1))
        block[4] = jnp.concatenate(
            [
                tensor_move(block[2][:, :half], along_z(-2)),
                tensor_move(block[-2][:, half:], along_z(2)),
            ],
            axis=1,
        )
        order = (0, 1, -1, 2, -2, 3, -3, 4)
        near = jnp.concatenate([block[k] for k in order[:5]], axis=0)
        far = jnp.concatenate([block[k] for k in order[5:]], axis=0)
        rows = jnp.concatenate(
            [near, far, tensor_move(near, CORE), tensor_move(far, CORE)], axis=0
        )
        early, rows, late = lax.optimization_barrier((early, rows, late))

    with jax.named_scope("hidden"):
        late = to_groups(late)
        depth = gate_w.shape[1]
        early = early.reshape(expert_count, -1, width)
        hidden = swiglu(rows, early, depth)

        hidden = hidden.reshape(2, 8, 2, capacity, -1)
        mine, others = ([part[:, n].reshape(8 * capacity, -1) for n in (0, 1)] for part in hidden)
        late, mine, others = lax.optimization_barrier((late, mine, others))
        late = late.reshape(expert_count, -1, width)
        down_own = jnp.concatenate([early[:, 2 * depth :], late], axis=1).reshape(-1, width)

    with jax.named_scope("down"):
        theirs = [
            jnp.dot(rows, down_own, preferred_element_type=jnp.float32).astype(bf16)
            for rows in others
        ]
        received = [tensor_move(t, CORE) for t in theirs]
        mine, _ = lax.optimization_barrier((mine, theirs))
        totals = []
        for rows, got in zip(mine, received):
            here = jnp.dot(rows, down_own, preferred_element_type=jnp.float32)
            totals.append((here + got.astype(jnp.float32)).astype(bf16))

    def chains(total, longer, flip):
        part = {k: total[i * capacity : (i + 1) * capacity] for i, k in enumerate(order)}
        stay = tensor_move(part[0], X_LO) if flip else part[0]
        far = tensor_move(part[4], along_z(longer))
        near = tensor_move(part[-3 * longer], along_z(-longer))
        far = tensor_move(add(far, part[3 * longer]).astype(bf16), along_z(longer))
        near = tensor_move(add(near, part[-2 * longer]).astype(bf16), along_z(-longer))
        far = tensor_move(add(far, part[2 * longer]).astype(bf16), along_z(longer))
        near = tensor_move(add(near, part[-longer]).astype(bf16), along_z(-longer, flip))
        far = tensor_move(add(far, part[longer]).astype(bf16), along_z(longer, flip))
        return add(stay, near) + far.astype(jnp.float32)

    with jax.named_scope("scatter"):
        summed = chains(totals[1], -1, 2) + chains(totals[0], 1, 0)
        outs = [summed.astype(bf16)]

    with jax.named_scope("mix"):
        scaled = onehot * weight[:, None, :]
        expert_out = jnp.concatenate(outs, axis=1)
        copies = jnp.broadcast_to(expert_out[None], (expert_count,) + expert_out.shape)
        return lax.dot_general(
            scaled.reshape(-1, tok_rows),
            to_groups(copies).astype(jnp.float32),
            (((0,), (0,)), ((), ())),
            precision=lax.Precision.HIGHEST,
            preferred_element_type=jnp.float32,
        ).astype(bf16)


def solution(mesh):
    placed = (
        P("tensor", None),
        P("tensor", None),
        P("tensor", None),
        P(None, ("expert", "tensor"), None),
        P(None, ("expert", "tensor"), None),
        P(None, ("expert", "tensor"), None),
    )
    return jax.shard_map(
        per_device, mesh=mesh, in_specs=placed, out_specs=P("tensor", None), check_vma=False
    )
```
